32 devices in a mesh: expert: 16 (over z, y, x), tp: 2 (over core).
Axes of the slice: x: 2, y: 2, z: 4, core: 2. Of those that a mesh axis runs over, the one named last changes fastest.
Arguments:
- tokens: bfloat16 [1024, 2880], P(('expert', 'tp')), may hold values from -6 to 6
- expert_ids: int32 [1024, 4], P(('expert', 'tp')), may hold values from 0 to 15, all different within a row; in each aligned block of 32 rows (0 to 31, 32 to 63, ...) at most 16 rows name the same one
- route_logits: float32 [1024, 4], P(('expert', 'tp')), may hold values from -4 to 4
- gate_weight: bfloat16 [16, 2880, 1440], P('expert', None, 'tp'), may hold values from -0.109375 to 0.109375
- up_weight: bfloat16 [16, 2880, 1440], P('expert', None, 'tp'), may hold values from -0.109375 to 0.109375
- down_weight: bfloat16 [16, 1440, 2880], P('expert', 'tp'), may hold values from -0.15625 to 0.15625
Outputs:
- mixed_out: bfloat16 [1024, 2880], P(('expert', 'tp'))
The draws below stay inside these ranges and needn't reach their ends.
Inputs may be any that keep to these rules, and one draw needn't show every extreme that they name: `expert_ids`: within each aligned block of 32 tokens (the tokens of one device) every token names 4 different experts and no expert is named more than 16 times; in every draw some expert is named exactly 16 times in some block.
All inputs are finite; a program needn't handle non-finite values.
Results may differ from the reference program's by a relative error of at most 0.0058.
Values may be sent and summed in bfloat16 or wider, within the bound.
A program may use at most 128 MiB of HBM per device.

```python
import math
import jax
import jax.numpy as jnp
import numpy as np
from jax import lax

D = 2880
HIDDEN_SIZE = 1440
TOP = 4
TOK_DEV = 32
EXPERTS = 16
CAP = 16
TOKENS = 1024


def level_of(stream_key, extent, pieces, smallest, largest):
    factor_of = 1.0
    for dim, blocks in pieces:
        draws = jax.random.uniform(jax.random.fold_in(jax.random.fold_in(stream_key, 6), dim), (blocks,), jnp.float32, smallest / len(pieces), largest / len(pieces))
        factor_of = factor_of * jnp.repeat(jnp.exp(draws), extent[dim] // blocks).reshape((-1,) + (1,) * (len(extent) - 1 - dim))
    return factor_of


def assign_block(own_key, own, number, rows, count, top, reach, lean):
    ranking = jax.random.permutation(own_key, count)
    crowded, common = shares(count, rows * top, reach, lean, True), shares(count, rows * top, reach, lean, False)
    places = jnp.arange(count)

    def named(lengths, rotation):
        used = int((lengths > 0).sum())
        fixed = max(1, used // 4)
        moved = fixed + (places - fixed + rotation * (used - fixed)) % max(1, count - fixed)
        return jnp.zeros((count,), jnp.int32).at[ranking[jnp.where(places < fixed, places, moved)]].set(jnp.asarray(lengths, jnp.int32))

    lengths = jnp.where(number % 4 == 0, named(crowded, number // 4), named(common, number - number // 4 - 1))
    mixed = jax.random.permutation(jax.random.fold_in(own, 3), count)
    donor, receiver = mixed[0:count // 2 * 2:2], mixed[1:count // 2 * 2:2]
    slack = jnp.minimum(lengths[donor] - 1, reach - lengths[receiver]) // 2
    slack = jnp.where((donor == ranking[0]) | (receiver == ranking[0]) | (lengths[receiver] == 0), 0, jnp.maximum(slack, 0))
    moved = jax.random.randint(jax.random.fold_in(own, 4), (count // 2,), 0, 1 << 20) % (slack + 1)
    lengths = lengths.at[donor].add(-moved).at[receiver].add(moved)
    labels = jnp.searchsorted(jnp.cumsum(lengths), jnp.arange(rows * top), side="right").astype(jnp.int32)
    listing = labels.reshape(top, rows).T
    listing = listing[jax.random.permutation(jax.random.fold_in(own, 1), rows)]
    rotation = jax.random.randint(jax.random.fold_in(own, 2), (rows, 1), 0, top)
    return jnp.take_along_axis(listing, (jnp.arange(top)[None, :] + rotation) % top, axis=1)


def shares(count, total, bound, slope, full):
    loads = [(1 << 20) // math.isqrt(grade ** slope) + 1 for grade in range(1, count + 1)]
    largest = bound if full else min(bound, max(-(-total // count), total * loads[0] // sum(loads)))
    least = 1 if total - largest >= count - 1 else 0
    counts, rest = [largest] + [least] * (count - 1), total - largest - least * (count - 1)
    while rest > 0:
        candidates = [i for i in range(1, count) if counts[i] < largest] or [i for i in range(1, count) if counts[i] < bound]
        pool, remaining = sum([loads[i] for i in candidates]), rest
        for i in candidates:
            more = min(bound - counts[i], max(1, remaining * loads[i] // pool), rest)
            counts[i] = counts[i] + more
            rest = rest - more
    return np.array(counts)


def noise(rng, extent, spread, limit, split=(), kind=jnp.bfloat16):
    values = jax.random.normal(rng, extent, jnp.float32) * spread
    if len(split) > 0:
        values = level_of(rng, extent, split, -0.22, 0.18) * values
    return jnp.clip(values, min=-limit, max=limit).astype(kind)


def setup_inputs(seed: int = 0) -> dict:
    key_of = jax.random.split(jax.random.key(seed), 7)
    tokens = noise(key_of[0], (TOKENS, D), 1.0, 6.0, ((0, 32),))
    expert_ids_keys = jax.random.split(jax.random.fold_in(key_of[1], 1), TOKENS // TOK_DEV)
    expert_ids_turns = jax.random.permutation(jax.random.fold_in(key_of[1], 3), TOKENS // TOK_DEV)
    expert_ids = jax.vmap(lambda own, number: assign_block(jax.random.fold_in(key_of[1], 2), own, number, TOK_DEV, EXPERTS, TOP, CAP, 2))(expert_ids_keys, expert_ids_turns).reshape((TOKENS, TOP))
    route_logits = noise(key_of[2], (TOKENS, TOP), 1.5, 4.0, ((0, 32),), jnp.float32)
    gate_weight = noise(key_of[3], (EXPERTS, D, HIDDEN_SIZE), D ** -0.5, 0.109375, ((0, 16), (2, 2)))
    up_weight = noise(key_of[4], (EXPERTS, D, HIDDEN_SIZE), D ** -0.5, 0.109375, ((0, 16), (2, 2)))
    down_weight = noise(key_of[5], (EXPERTS, HIDDEN_SIZE, D), HIDDEN_SIZE ** -0.5, 0.15625, ((0, 16), (1, 2)))
    return dict(tokens=tokens, expert_ids=expert_ids, route_logits=route_logits, gate_weight=gate_weight, up_weight=up_weight, down_weight=down_weight)


def reference(tokens, expert_ids, route_logits, gate_weight, up_weight, down_weight):
    block_count = TOKENS // TOK_DEV
    block_picks = expert_ids.reshape(block_count, TOK_DEV * TOP)
    expert_range = jnp.arange(EXPERTS, dtype=jnp.int32)
    one_hot = (block_picks[:, :, None] == expert_range[None, None, :]).astype(jnp.int32)
    earlier = jnp.cumsum(one_hot, axis=1) - one_hot
    slot_index = jnp.sum(earlier * one_hot, axis=2).astype(jnp.int32)
    block_index = jnp.arange(block_count, dtype=jnp.int32)[:, None]
    position = (block_picks * (block_count * CAP) + block_index * CAP + slot_index).astype(jnp.int32)
    token_index = jnp.broadcast_to(jnp.arange(TOKENS, dtype=jnp.int32).reshape(block_count, TOK_DEV, 1), (block_count, TOK_DEV, TOP)).reshape(-1)
    table = jnp.full((EXPERTS * block_count * CAP,), TOKENS, dtype=jnp.int32)
    table = table.at[position.reshape(-1)].set(token_index).reshape(EXPERTS, block_count * CAP)
    padded = jnp.concatenate([tokens, jnp.zeros((1, D), tokens.dtype)], axis=0)

    def run_expert(packed):
        table_row, gate_local, up_local, down_local = packed
        row_block = padded[table_row]
        gate_act = jnp.dot(row_block, gate_local, preferred_element_type=jnp.float32)
        up_act = jnp.dot(row_block, up_local, preferred_element_type=jnp.float32)
        hidden = (gate_act * jax.nn.sigmoid(1.702 * gate_act) * (up_act + 1.0)).astype(jnp.bfloat16)
        return jnp.dot(hidden, down_local, preferred_element_type=jnp.float32).astype(jnp.bfloat16)

    outputs = lax.map(run_expert, (table, gate_weight, up_weight, down_weight))
    flat_out = outputs.reshape(EXPERTS * block_count * CAP, D)
    picked = flat_out[position.reshape(TOKENS, TOP)]
    scores = jnp.exp(route_logits.astype(jnp.float32))
    weights = scores / jnp.sum(scores, axis=1, keepdims=True)
    mixed_out = jnp.sum(weights[:, :, None] * picked.astype(jnp.float32), axis=1)
    return mixed_out.astype(jnp.bfloat16)
```

```python
import functools

import jax
import jax.numpy as jnp
from jax import lax
from jax.experimental import pallas as pl
from jax.experimental.pallas import tpu as pltpu
from jax.sharding import PartitionSpec as P

MESH = pl.DeviceIdType.MESH
F32 = jnp.float32
BF16 = jnp.bfloat16


def flip(a, b, extent):
    total, bit = 0, 1
    while bit < extent:
        total = total + ((a // bit + b // bit) % 2) * bit
        bit *= 2
    return total


def moe_kernel(
    sizes,
    tok_ref, ids_ref, logit_ref, gate_hbm, up_hbm, down_hbm,
    out_ref,
    zbuf, xs, xr, gate_w, up_w, down_w, part, tbuf, trecv, ybuf, yrecv, cbuf, crecv, acc,
    wsem, zsend_sem, zrecv_sem, xsend_sem, xrecv_sem, fsend_sem, frecv_sem,
    tsend_sem, trecv_sem, ysend_sem, yrecv_sem, csend_sem, crecv_sem,
):
    outer, inner, cap, picks, width, wide = sizes
    tok_count = tok_ref.shape[0]
    group = inner * cap
    e, c = lax.axis_index("expert"), lax.axis_index("tp")
    z, p = e // inner, e % inner
    other = 1 - c

    loads = [
        pltpu.make_async_copy(gate_hbm.at[0], gate_w.at[pl.ds(0, width)], wsem.at[0]),
        pltpu.make_async_copy(up_hbm.at[0], up_w.at[pl.ds(0, width)], wsem.at[1]),
        pltpu.make_async_copy(down_hbm.at[0], down_w, wsem.at[2]),
    ]
    for load in loads:
        load.start()

    barrier = pltpu.get_barrier_semaphore()
    for d in range(1, outer):
        pl.semaphore_signal(barrier, inc=1, device_id=(flip(z, d, outer) * inner + p, c), device_id_type=MESH)
    for d in range(1, inner):
        pl.semaphore_signal(barrier, inc=1, device_id=(z * inner + flip(p, d, inner), c), device_id_type=MESH)
    pl.semaphore_signal(barrier, inc=1, device_id=(e, other), device_id_type=MESH)

    experts = outer * inner
    ids = ids_ref[...]
    expert_lane = lax.broadcasted_iota(jnp.int32, (tok_count, experts), 1)
    named = [(ids[:, k : k + 1] == expert_lane).astype(F32) for k in range(picks)]
    lower = (
        lax.broadcasted_iota(jnp.int32, (tok_count, tok_count), 1)
        < lax.broadcasted_iota(jnp.int32, (tok_count, tok_count), 0)
    ).astype(F32)
    earlier = jnp.dot(lower, sum(named), preferred_element_type=F32)
    scores = jnp.exp(logit_ref[...])
    weights = scores / jnp.sum(scores, axis=1, keepdims=True)
    tail = tok_ref[:, wide - 128 :].astype(F32)
    lane = lax.broadcasted_iota(jnp.int32, (tok_count, 128), 1)
    first = 128 - 4 * picks
    for k in range(picks):
        slot = jnp.sum(earlier * named[k], axis=1, keepdims=True)
        weight = weights[:, k : k + 1]
        high = weight.astype(BF16).astype(F32)
        for j, value in enumerate((ids[:, k : k + 1].astype(F32), slot, high, weight - high)):
            tail = jnp.where(lane == first + 4 * k + j, value, tail)
    zbuf[0, :, : wide - 128] = tok_ref[:, : wide - 128]
    zbuf[0, :, wide - 128 :] = tail.astype(BF16)
    gate_w[width:, :] = jnp.zeros((wide - width, gate_w.shape[1]), BF16)
    up_w[width:, :] = jnp.zeros((wide - width, up_w.shape[1]), BF16)

    pl.semaphore_wait(barrier, outer + inner - 1)

    def z_copy(s):
        return pltpu.make_async_remote_copy(
            src_ref=zbuf.at[0], dst_ref=zbuf.at[s], send_sem=zsend_sem.at[s], recv_sem=zrecv_sem.at[s],
            device_id=(flip(z, s, outer) * inner + p, c), device_id_type=MESH,
        )

    def x_copy(s, d, receive=False):
        peer = flip(p, d, inner)
        return pltpu.make_async_remote_copy(
            src_ref=xs.at[s, peer], dst_ref=xr.at[s, c, peer if receive else p],
            send_sem=xsend_sem.at[s, d], recv_sem=xrecv_sem.at[s, d],
            device_id=(z * inner + peer, c), device_id_type=MESH,
        )

    def f_copy(s, d, receive=False):
        peer = flip(p, d, inner)
        return pltpu.make_async_remote_copy(
            src_ref=xr.at[s, c, peer], dst_ref=xr.at[s, other if receive else c, peer],
            send_sem=fsend_sem.at[s, d], recv_sem=frecv_sem.at[s, d],
            device_id=(e, other), device_id_type=MESH,
        )

    def t_copy(s):
        return pltpu.make_async_remote_copy(
            src_ref=tbuf.at[s], dst_ref=trecv.at[s], send_sem=tsend_sem.at[s], recv_sem=trecv_sem.at[s],
            device_id=(e, other), device_id_type=MESH,
        )

    def y_copy(s, d, receive=False):
        peer = flip(p, d, inner)
        return pltpu.make_async_remote_copy(
            src_ref=ybuf.at[s, peer], dst_ref=yrecv.at[s, peer if receive else p],
            send_sem=ysend_sem.at[s, d], recv_sem=yrecv_sem.at[s, d],
            device_id=(z * inner + peer, c), device_id_type=MESH,
        )

    def c_copy(s):
        return pltpu.make_async_remote_copy(
            src_ref=cbuf.at[s], dst_ref=crecv.at[s], send_sem=csend_sem.at[s], recv_sem=crecv_sem.at[s],
            device_id=(flip(z, s, outer) * inner + p, c), device_id_type=MESH,
        )

    def notes(s):
        told = zbuf[s, :, wide - 128 :].astype(F32)
        found = []
        for k in range(picks):
            at = first + 4 * k
            row = told[:, at : at + 1] * cap + told[:, at + 1 : at + 2] - (z * group).astype(F32)
            found.append((row, told[:, at + 2 : at + 3], told[:, at + 3 : at + 4]))
        return found

    def slots():
        return lax.broadcasted_iota(jnp.int32, (tok_count, group), 1).astype(F32)

    def dispatch(s):
        rows = slots()
        placing = sum((row == rows).astype(F32) for row, _, _ in notes(s)).astype(BF16)
        packed = lax.dot_general(placing, zbuf[s], (((0,), (0,)), ((), ())), preferred_element_type=F32)
        xs[s] = packed.astype(BF16).reshape(inner, cap, wide)
        for d in range(1, inner):
            x_copy(s, d).start()
        xr[s, c, p] = xs[s, p]
        f_copy(s, 0).start()

    def compute(s):
        rows = xr[s].reshape(2 * group, wide)
        gate_act = jnp.dot(rows, gate_w[...], preferred_element_type=F32)
        up_act = jnp.dot(rows, up_w[...], preferred_element_type=F32)
        hidden = (gate_act * jax.nn.sigmoid(1.702 * gate_act) * (up_act + 1.0)).astype(BF16)
        part[s % 2] = jnp.dot(hidden, down_w[...], preferred_element_type=F32).reshape(2, group, width)
        tbuf[s] = part[s % 2, other].astype(BF16)
        t_copy(s).start()

    def give_back(s):
        t_copy(s).wait_recv()
        whole = part[s % 2, c] + trecv[s].astype(F32)
        ybuf[s] = whole.astype(BF16).reshape(inner, cap, width)
        for d in range(1, inner):
            y_copy(s, d).start()
        yrecv[s, p] = ybuf[s, p]

    def combine(s):
        for d in range(1, inner):
            y_copy(s, d, True).wait_recv()
        rows = slots()
        high = jnp.zeros((tok_count, group), F32)
        low = jnp.zeros((tok_count, group), F32)
        for row, weight_high, weight_low in notes(s):
            high = high + jnp.where(row == rows, weight_high, 0.0)
            low = low + jnp.where(row == rows, weight_low, 0.0)
        mixing = jnp.concatenate([high, low], axis=0).astype(BF16)
        both = jnp.dot(mixing, yrecv[s].reshape(group, width), preferred_element_type=F32)
        return both[:tok_count] + both[tok_count:]

    for s in range(1, outer):
        z_copy(s).start()
    dispatch(0)
    for load in loads:
        load.wait()

    def step(i, carry):
        @pl.when(i + 1 < outer)
        def _():
            z_copy(i + 1).wait_recv()
            dispatch(i + 1)

        @pl.when(i < outer)
        def _():
            for d in range(1, inner):
                x_copy(i, d, True).wait_recv()
                f_copy(i, d).start()
            for d in range(inner):
                f_copy(i, d, True).wait_recv()
            compute(i)

        @pl.when((i >= 1) & (i <= outer))
        def _():
            give_back(i - 1)

        @pl.when(i == 2)
        def _():
            acc[...] = combine(0)

        @pl.when(i > 2)
        def _():
            cbuf[i - 2] = combine(i - 2).astype(BF16)
            c_copy(i - 2).start()

        return carry

    lax.fori_loop(0, outer + 2, step, 0)

    total = acc[...]
    for s in range(1, outer):
        c_copy(s).wait_recv()
        total = total + crecv[s].astype(F32)
    out_ref[...] = total.astype(BF16)

    for s in range(outer):
        for d in range(1, inner):
            x_copy(s, d).wait_send()
            y_copy(s, d).wait_send()
        for d in range(inner):
            f_copy(s, d).wait_send()
        t_copy(s).wait_send()
        if s > 0:
            z_copy(s).wait_send()
            c_copy(s).wait_send()


def split_of(experts):
    inner = 1
    while 4 * inner * inner <= experts:
        inner *= 2
    return experts // inner, inner


def fused_plan(mesh, tokens, expert_ids, gate_weight):
    experts, cores = mesh.shape["expert"], mesh.shape["tp"]
    tok_dev, width = tokens.shape
    picks, half = expert_ids.shape[1], gate_weight.shape[2]
    cap = 2 * tok_dev * picks // experts
    outer, inner = split_of(experts)
    wide = -(-(width + 4 * picks) // 128) * 128
    if cores != 2 or outer * inner != experts or experts & (experts - 1) or experts > 256:
        return None
    if cap % 16 or tok_dev % 16 or tok_dev > 256 or width % 16 or half % 16:
        return None
    rows = outer * inner * cap
    lanes = -(-half // 128) * 128
    held = 2 * wide * (2 * lanes + half + 7 * rows + 3 * outer * tok_dev) + 16 * wide * inner * cap
    if held > 44 * 2**20:
        return None
    return outer, inner, cap, picks, width, wide


def fused(sizes, tokens, expert_ids, route_logits, gate_weight, up_weight, down_weight):
    outer, inner, cap, picks, width, wide = sizes
    tok_dev = tokens.shape[0]
    half = gate_weight.shape[2]
    group = inner * cap
    padded = jnp.pad(tokens, ((0, 0), (0, wide - width)))
    vmem, hbm = pl.BlockSpec(memory_space=pltpu.VMEM), pl.BlockSpec(memory_space=pl.ANY)
    dma = pltpu.SemaphoreType.DMA
    rows = 2 * outer * group
    return pl.pallas_call(
        functools.partial(moe_kernel, sizes),
        out_shape=jax.ShapeDtypeStruct((tok_dev, width), BF16),
        in_specs=[vmem, vmem, vmem, hbm, hbm, hbm],
        out_specs=vmem,
        scratch_shapes=[
            pltpu.VMEM((outer, tok_dev, wide), BF16),
            pltpu.VMEM((outer, inner, cap, wide), BF16),
            pltpu.VMEM((outer, 2, inner, cap, wide), BF16),
            pltpu.VMEM((wide, half), BF16),
            pltpu.VMEM((wide, half), BF16),
            pltpu.VMEM((half, width), BF16),
            pltpu.VMEM((2, 2, group, width), F32),
            pltpu.VMEM((outer, group, width), BF16),
            pltpu.VMEM((outer, group, width), BF16),
            pltpu.VMEM((outer, inner, cap, width), BF16),
            pltpu.VMEM((outer, inner, cap, width), BF16),
            pltpu.VMEM((outer, tok_dev, width), BF16),
            pltpu.VMEM((outer, tok_dev, width), BF16),
            pltpu.VMEM((tok_dev, width), F32),
            dma((3,)),
            dma((outer,)), dma((outer,)),
            dma((outer, inner)), dma((outer, inner)),
            dma((outer, inner)), dma((outer, inner)),
            dma((outer,)), dma((outer,)),
            dma((outer, inner)), dma((outer, inner)),
            dma((outer,)), dma((outer,)),
        ],
        compiler_params=pltpu.CompilerParams(
            collective_id=0, has_side_effects=True, vmem_limit_bytes=56 * 2**20
        ),
        cost_estimate=pl.CostEstimate(
            flops=6 * rows * width * half, bytes_accessed=6 * width * half, transcendentals=rows * half
        ),
    )(padded, expert_ids, route_logits, gate_weight, up_weight, down_weight)


def plain(tokens, expert_ids, route_logits, gate_weight, up_weight, down_weight):
    experts = lax.axis_size("expert")
    tok_dev, model_width = tokens.shape
    pick_count = expert_ids.shape[1]
    capacity = 2 * tok_dev * pick_count // experts
    flat_ids = expert_ids.reshape(-1)
    pick_range = jnp.arange(flat_ids.shape[0], dtype=jnp.int32)
    same = (flat_ids[:, None] == flat_ids[None, :]) & (pick_range[None, :] < pick_range[:, None])
    slot_index = jnp.sum(same.astype(jnp.int32), axis=1)
    position = flat_ids * capacity + slot_index
    slot_range = jnp.arange(experts * capacity, dtype=jnp.int32)
    matches = (position[:, None] == slot_range[None, :]).astype(jnp.int32)
    placing = jnp.sum(matches.reshape(tok_dev, pick_count, -1), axis=1).astype(jnp.bfloat16)
    outgoing = lax.dot_general(
        placing, tokens, (((0,), (0,)), ((), ())), preferred_element_type=jnp.float32
    )
    outgoing = outgoing.astype(jnp.bfloat16).reshape(experts, capacity, model_width)
    gate_local = gate_weight[0]
    up_local = up_weight[0]
    down_local = down_weight[0]
    received = lax.all_to_all(outgoing, "expert", split_axis=0, concat_axis=0, tiled=True)
    items = received.shape[1]
    row_total = experts * items
    row_block = received.reshape(row_total, model_width)
    paired = lax.all_gather(row_block, "tp", axis=0, tiled=True)
    gate_act = jnp.dot(paired, gate_local, preferred_element_type=jnp.float32)
    up_act = jnp.dot(paired, up_local, preferred_element_type=jnp.float32)
    hidden = (gate_act * jax.nn.sigmoid(1.702 * gate_act) * (up_act + 1.0)).astype(jnp.bfloat16)
    summed = lax.psum_scatter(
        jnp.dot(hidden, down_local, preferred_element_type=jnp.float32),
        "tp",
        scatter_dimension=0,
        tiled=True,
    )
    results = summed.astype(jnp.bfloat16).reshape(experts, items, model_width)
    returned = lax.all_to_all(results, "expert", split_axis=0, concat_axis=0, tiled=True).reshape(
        experts * capacity, model_width
    )
    picked = returned[position.reshape(tok_dev, pick_count)]
    scores = jnp.exp(route_logits)
    weights = scores / jnp.sum(scores, axis=1, keepdims=True)
    mixed_out = jnp.sum(weights[:, :, None] * picked.astype(jnp.float32), axis=1)
    return mixed_out.astype(jnp.bfloat16)


def solution(mesh):
    def body(tokens, expert_ids, route_logits, gate_weight, up_weight, down_weight):
        sizes = fused_plan(mesh, tokens, expert_ids, gate_weight)
        run = plain if sizes is None else functools.partial(fused, sizes)
        return run(tokens, expert_ids, route_logits, gate_weight, up_weight, down_weight)

    placed = (
        P(("expert", "tp"), None),
        P(("expert", "tp"), None),
        P(("expert", "tp"), None),
        P("expert", None, "tp"),
        P("expert", None, "tp"),
        P("expert", "tp", None),
    )
    return jax.shard_map(
        body, mesh=mesh, in_specs=placed, out_specs=P(("expert", "tp"), None), check_vma=False
    )
```

```python
import functools

import jax
import jax.numpy as jnp
from jax import lax
from jax.experimental import pallas as pl
from jax.experimental.pallas import tpu as pltpu
from jax.sharding import PartitionSpec as P

MESH = pl.DeviceIdType.MESH
F32 = jnp.float32
BF16 = jnp.bfloat16


def flip(a, b, extent):
    total, bit = 0, 1
    while bit < extent:
        total = total + ((a // bit + b // bit) % 2) * bit
        bit *= 2
    return total


def moe_kernel(
    sizes,
    tok_ref, ids_ref, logit_ref, gate_hbm, up_hbm, down_hbm,
    out_ref,
    zbuf, xs, xr, gate_w, up_w, down_w, part, tbuf, trecv, ybuf, yrecv, cbuf, crecv, acc,
    wsem, zsend_sem, zrecv_sem, xsend_sem, xrecv_sem, fsend_sem, frecv_sem,
    tsend_sem, trecv_sem, ysend_sem, yrecv_sem, csend_sem, crecv_sem,
):
    outer, inner, cap, picks, width, wide = sizes
    tok_count = tok_ref.shape[0]
    group = inner * cap
    e, c = lax.axis_index("expert"), lax.axis_index("tp")
    z, p = e // inner, e % inner
    other = 1 - c

    loads = [
        pltpu.make_async_copy(gate_hbm.at[0], gate_w, wsem.at[0]),
        pltpu.make_async_copy(up_hbm.at[0], up_w, wsem.at[1]),
        pltpu.make_async_copy(down_hbm.at[0], down_w, wsem.at[2]),
    ]
    for load in loads:
        load.start()

    barrier = pltpu.get_barrier_semaphore()
    for d in range(1, outer):
        pl.semaphore_signal(barrier, inc=1, device_id=((z + d) % outer * inner + p, c), device_id_type=MESH)
    for d in range(1, inner):
        pl.semaphore_signal(barrier, inc=1, device_id=(z * inner + flip(p, d, inner), c), device_id_type=MESH)
    pl.semaphore_signal(barrier, inc=1, device_id=(e, other), device_id_type=MESH)

    experts = outer * inner
    expert_lane = lax.broadcasted_iota(jnp.int32, (tok_count, experts), 1)
    square = (tok_count, tok_count)
    row_at, lane_at = lax.broadcasted_iota(jnp.int32, square, 0), lax.broadcasted_iota(jnp.int32, square, 1)

    def upright(line):
        return jnp.sum(jnp.where(row_at == lane_at, line, jnp.zeros_like(line)), axis=1, keepdims=True)

    chosen = [upright(ids_ref[k : k + 1, :]) for k in range(picks)]
    named = [(column == expert_lane).astype(F32) for column in chosen]
    lower = (lane_at < row_at).astype(F32)
    earlier = jnp.dot(lower, sum(named), preferred_element_type=F32)
    scores = jnp.exp(logit_ref[...])
    weights = scores / jnp.sum(scores, axis=0, keepdims=True)
    zbuf[z, :, wide - 128 :] = jnp.zeros((tok_count, 128), BF16)
    zbuf[z, :, :width] = tok_ref[...]
    tail = zbuf[z, :, wide - 128 :].astype(F32)
    lane = lax.broadcasted_iota(jnp.int32, (tok_count, 128), 1)
    first = 128 - 4 * picks
    for k in range(picks):
        slot = jnp.sum(earlier * named[k], axis=1, keepdims=True)
        weight = upright(weights[k : k + 1, :])
        high = weight.astype(BF16).astype(F32)
        for j, value in enumerate((chosen[k].astype(F32), slot, high, weight - high)):
            tail = jnp.where(lane == first + 4 * k + j, value, tail)
    zbuf[z, :, wide - 128 :] = tail.astype(BF16)

    pl.semaphore_wait(barrier, outer + inner - 1)

    def origin(s):
        near = jnp.minimum(z, outer - 1 - z)
        toward = jnp.where(2 * z < outer, -1, 1)
        j = (s + 1) // 2
        paired = jnp.where(s % 2 == 1, toward * j, -toward * j)
        return z + jnp.where(s <= 2 * near, paired, -toward * (s - near))

    def z_copy(block, way):
        return pltpu.make_async_remote_copy(
            src_ref=zbuf.at[block], dst_ref=zbuf.at[block],
            send_sem=zsend_sem.at[way, block], recv_sem=zrecv_sem.at[block],
            device_id=((z + 2 * way - 1) * inner + p, c), device_id_type=MESH,
        )

    def pass_on(d):
        @pl.when(z >= d)
        def _():
            z_copy(z - d, 1).wait_recv()

            @pl.when(z + 1 < outer)
            def _():
                z_copy(z - d, 1).start()

        @pl.when(z + d < outer)
        def _():
            z_copy(z + d, 0).wait_recv()

            @pl.when(z > 0)
            def _():
                z_copy(z + d, 0).start()

    def x_copy(s, d, receive=False):
        peer = flip(p, d, inner)
        return pltpu.make_async_remote_copy(
            src_ref=xs.at[s, peer], dst_ref=xr.at[s, c, peer if receive else p],
            send_sem=xsend_sem.at[s, d], recv_sem=xrecv_sem.at[s, d],
            device_id=(z * inner + peer, c), device_id_type=MESH,
        )

    def f_copy(s, d, receive=False):
        peer = flip(p, d, inner)
        return pltpu.make_async_remote_copy(
            src_ref=xr.at[s, c, peer], dst_ref=xr.at[s, other if receive else c, peer],
            send_sem=fsend_sem.at[s, d], recv_sem=frecv_sem.at[s, d],
            device_id=(e, other), device_id_type=MESH,
        )

    def t_copy(s):
        return pltpu.make_async_remote_copy(
            src_ref=tbuf.at[s], dst_ref=trecv.at[s], send_sem=tsend_sem.at[s], recv_sem=trecv_sem.at[s],
            device_id=(e, other), device_id_type=MESH,
        )

    def y_copy(s, d, receive=False):
        peer = flip(p, d, inner)
        return pltpu.make_async_remote_copy(
            src_ref=ybuf.at[s, peer], dst_ref=yrecv.at[s, peer if receive else p],
            send_sem=ysend_sem.at[s, d], recv_sem=yrecv_sem.at[s, d],
            device_id=(z * inner + peer, c), device_id_type=MESH,
        )

    def c_copy(s, peer, receive=False):
        return pltpu.make_async_remote_copy(
            src_ref=cbuf.at[s], dst_ref=crecv.at[peer if receive else z],
            send_sem=csend_sem.at[s], recv_sem=crecv_sem.at[peer if receive else z],
            device_id=(peer * inner + p, c), device_id_type=MESH,
        )

    def notes(s):
        told = zbuf[origin(s), :, wide - 128 :].astype(F32)
        found = []
        for k in range(picks):
            at = first + 4 * k
            row = told[:, at : at + 1] * cap + told[:, at + 1 : at + 2] - (z * group).astype(F32)
            found.append((row, told[:, at + 2 : at + 3], told[:, at + 3 : at + 4]))
        return found

    def slots():
        return lax.broadcasted_iota(jnp.int32, (tok_count, group), 1).astype(F32)

    def dispatch(s):
        rows = slots()
        placing = sum((row == rows).astype(F32) for row, _, _ in notes(s)).astype(BF16)
        packed = lax.dot_general(placing, zbuf[origin(s)], (((0,), (0,)), ((), ())), preferred_element_type=F32)
        xs[s] = packed.astype(BF16).reshape(inner, cap, wide)
        for d in range(1, inner):
            x_copy(s, d).start()
        xr[s, c, p] = xs[s, p]
        f_copy(s, 0).start()

    def compute(s):
        rows = xr[s, :, :, :, :width].reshape(2 * group, width)
        across = (((1,), (1,)), ((), ()))
        gate_act = lax.dot_general(rows, gate_w[...], across, preferred_element_type=F32)
        up_act = lax.dot_general(rows, up_w[...], across, preferred_element_type=F32)
        hidden = (gate_act * jax.nn.sigmoid(1.702 * gate_act) * (up_act + 1.0)).astype(BF16)
        part[s % 2] = jnp.dot(hidden, down_w[...], preferred_element_type=F32).reshape(2, group, width)
        tbuf[s] = part[s % 2, other].astype(BF16)
        t_copy(s).start()

    def give_back(s):
        t_copy(s).wait_recv()
        whole = part[s % 2, c] + trecv[s].astype(F32)
        ybuf[s] = whole.astype(BF16).reshape(inner, cap, width)
        for d in range(1, inner):
            y_copy(s, d).start()
        yrecv[s, p] = ybuf[s, p]

    def combine(s):
        for d in range(1, inner):
            y_copy(s, d, True).wait_recv()
        rows = slots()
        high = jnp.zeros((tok_count, group), F32)
        low = jnp.zeros((tok_count, group), F32)
        for row, weight_high, weight_low in notes(s):
            high = high + jnp.where(row == rows, weight_high, 0.0)
            low = low + jnp.where(row == rows, weight_low, 0.0)
        mixing = jnp.concatenate([high, low], axis=0).astype(BF16)
        both = jnp.dot(mixing, yrecv[s].reshape(group, width), preferred_element_type=F32)
        return both[:tok_count] + both[tok_count:]

    @pl.when(z + 1 < outer)
    def _():
        z_copy(z, 1).start()

    @pl.when(z > 0)
    def _():
        z_copy(z, 0).start()

    dispatch(0)

    def step(i, carry):
        @pl.when(i + 1 < outer)
        def _():
            pass_on(i + 1)
            dispatch(i + 1)

        @pl.when((i >= 1) & (i <= outer))
        def _():
            give_back(i - 1)

        @pl.when(i == 2)
        def _():
            acc[...] = combine(0)

        @pl.when(i > 2)
        def _():
            cbuf[i - 2] = combine(i - 2).astype(BF16)
            c_copy(i - 2, origin(i - 2)).start()

        @pl.when(i < outer)
        def _():
            for d in range(1, inner):
                x_copy(i, d, True).wait_recv()
                f_copy(i, d).start()
            for d in range(inner):
                f_copy(i, d, True).wait_recv()

        @pl.when(i == 0)
        def _():
            for load in loads:
                load.wait()

        @pl.when(i < outer)
        def _():
            compute(i)

        return carry

    lax.fori_loop(0, outer + 2, step, 0)

    total = acc[...]
    for s in range(1, outer):
        peer = (z + s) % outer
        c_copy(s, peer, True).wait_recv()
        total = total + crecv[peer].astype(F32)
    out_ref[...] = total.astype(BF16)

    for s in range(outer):
        for d in range(1, inner):
            x_copy(s, d).wait_send()
            y_copy(s, d).wait_send()
        for d in range(inner):
            f_copy(s, d).wait_send()
        t_copy(s).wait_send()
        if s > 0:
            c_copy(s, origin(s)).wait_send()

        @pl.when((s <= z) & (z + 1 < outer))
        def _():
            z_copy(s, 1).wait_send()

        @pl.when((s >= z) & (z > 0))
        def _():
            z_copy(s, 0).wait_send()


def split_of(experts):
    inner = 1
    while 4 * inner * inner <= experts:
        inner *= 2
    return experts // inner, inner


def fused_plan(mesh, tokens, expert_ids, gate_weight):
    experts, cores = mesh.shape["expert"], mesh.shape["tp"]
    tok_dev, width = tokens.shape
    picks, half = expert_ids.shape[1], gate_weight.shape[2]
    cap = 2 * tok_dev * picks // experts
    outer, inner = split_of(experts)
    wide = -(-(width + 4 * picks) // 128) * 128
    if cores != 2 or outer * inner != experts or experts & (experts - 1) or experts > 256:
        return None
    if cap % 16 or tok_dev % 16 or tok_dev > 256 or width % 16 or half % 16:
        return None
    rows = outer * inner * cap
    held = 2 * wide * (3 * half + 7 * rows + 3 * outer * tok_dev) + 16 * wide * inner * cap
    if held > 44 * 2**20:
        return None
    return outer, inner, cap, picks, width, wide


def fused(sizes, tokens, expert_ids, route_logits, gate_weight, up_weight, down_weight):
    outer, inner, cap, picks, width, wide = sizes
    tok_dev = tokens.shape[0]
    half = gate_weight.shape[2]
    group = inner * cap
    gate, up = gate_weight.swapaxes(1, 2), up_weight.swapaxes(1, 2)
    vmem, hbm = pl.BlockSpec(memory_space=pltpu.VMEM), pl.BlockSpec(memory_space=pl.ANY)
    dma = pltpu.SemaphoreType.DMA
    rows = 2 * outer * group
    return pl.pallas_call(
        functools.partial(moe_kernel, sizes),
        out_shape=jax.ShapeDtypeStruct((tok_dev, width), BF16),
        in_specs=[vmem, vmem, vmem, hbm, hbm, hbm],
        out_specs=vmem,
        scratch_shapes=[
            pltpu.VMEM((outer, tok_dev, wide), BF16),
            pltpu.VMEM((outer, inner, cap, wide), BF16),
            pltpu.VMEM((outer, 2, inner, cap, wide), BF16),
            pltpu.VMEM((half, width), BF16),
            pltpu.VMEM((half, width), BF16),
            pltpu.VMEM((half, width), BF16),
            pltpu.VMEM((2, 2, group, width), F32),
            pltpu.VMEM((outer, group, width), BF16),
            pltpu.VMEM((outer, group, width), BF16),
            pltpu.VMEM((outer, inner, cap, width), BF16),
            pltpu.VMEM((outer, inner, cap, width), BF16),
            pltpu.VMEM((outer, tok_dev, width), BF16),
            pltpu.VMEM((outer, tok_dev, width), BF16),
            pltpu.VMEM((tok_dev, width), F32),
            dma((3,)),
            dma((2, outer)), dma((outer,)),
            dma((outer, inner)), dma((outer, inner)),
            dma((outer, inner)), dma((outer, inner)),
            dma((outer,)), dma((outer,)),
            dma((outer, inner)), dma((outer, inner)),
            dma((outer,)), dma((outer,)),
        ],
        compiler_params=pltpu.CompilerParams(
            collective_id=0, has_side_effects=True, vmem_limit_bytes=56 * 2**20
        ),
        cost_estimate=pl.CostEstimate(
            flops=6 * rows * width * half, bytes_accessed=6 * width * half, transcendentals=rows * half
        ),
    )(tokens, expert_ids.T, route_logits.T, gate, up, down_weight)


def plain(tokens, expert_ids, route_logits, gate_weight, up_weight, down_weight):
    experts = lax.axis_size("expert")
    tok_dev, model_width = tokens.shape
    pick_count = expert_ids.shape[1]
    capacity = 2 * tok_dev * pick_count // experts
    flat_ids = expert_ids.reshape(-1)
    pick_range = jnp.arange(flat_ids.shape[0], dtype=jnp.int32)
    same = (flat_ids[:, None] == flat_ids[None, :]) & (pick_range[None, :] < pick_range[:, None])
    slot_index = jnp.sum(same.astype(jnp.int32), axis=1)
    position = flat_ids * capacity + slot_index
    slot_range = jnp.arange(experts * capacity, dtype=jnp.int32)
    matches = (position[:, None] == slot_range[None, :]).astype(jnp.int32)
    placing = jnp.sum(matches.reshape(tok_dev, pick_count, -1), axis=1).astype(jnp.bfloat16)
    outgoing = lax.dot_general(
        placing, tokens, (((0,), (0,)), ((), ())), preferred_element_type=jnp.float32
    )
    outgoing = outgoing.astype(jnp.bfloat16).reshape(experts, capacity, model_width)
    gate_local = gate_weight[0]
    up_local = up_weight[0]
    down_local = down_weight[0]
    received = lax.all_to_all(outgoing, "expert", split_axis=0, concat_axis=0, tiled=True)
    items = received.shape[1]
    row_total = experts * items
    row_block = received.reshape(row_total, model_width)
    paired = lax.all_gather(row_block, "tp", axis=0, tiled=True)
    gate_act = jnp.dot(paired, gate_local, preferred_element_type=jnp.float32)
    up_act = jnp.dot(paired, up_local, preferred_element_type=jnp.float32)
    hidden = (gate_act * jax.nn.sigmoid(1.702 * gate_act) * (up_act + 1.0)).astype(jnp.bfloat16)
    summed = lax.psum_scatter(
        jnp.dot(hidden, down_local, preferred_element_type=jnp.float32),
        "tp",
        scatter_dimension=0,
        tiled=True,
    )
    results = summed.astype(jnp.bfloat16).reshape(experts, items, model_width)
    returned = lax.all_to_all(results, "expert", split_axis=0, concat_axis=0, tiled=True).reshape(
        experts * capacity, model_width
    )
    picked = returned[position.reshape(tok_dev, pick_count)]
    scores = jnp.exp(route_logits)
    weights = scores / jnp.sum(scores, axis=1, keepdims=True)
    mixed_out = jnp.sum(weights[:, :, None] * picked.astype(jnp.float32), axis=1)
    return mixed_out.astype(jnp.bfloat16)


def solution(mesh):
    def body(tokens, expert_ids, route_logits, gate_weight, up_weight, down_weight):
        sizes = fused_plan(mesh, tokens, expert_ids, gate_weight)
        run = plain if sizes is None else functools.partial(fused, sizes)
        return run(tokens, expert_ids, route_logits, gate_weight, up_weight, down_weight)

    placed = (
        P(("expert", "tp"), None),
        P(("expert", "tp"), None),
        P(("expert", "tp"), None),
        P("expert", None, "tp"),
        P("expert", None, "tp"),
        P("expert", "tp", None),
    )
    return jax.shard_map(
        body, mesh=mesh, in_specs=placed, out_specs=P(("expert", "tp"), None), check_vma=False
    )
```

```python
import functools

import jax
import jax.numpy as jnp
from jax import lax
from jax.experimental import pallas as pl
from jax.experimental.pallas import tpu as pltpu
from jax.sharding import PartitionSpec as P

MESH = pl.DeviceIdType.MESH
F32 = jnp.float32
BF16 = jnp.bfloat16


def flip(a, b, extent):
    total, bit = 0, 1
    while bit < extent:
        total = total + ((a // bit + b // bit) % 2) * bit
        bit *= 2
    return total


def moe_kernel(
    sizes,
    tok_ref, ids_ref, logit_ref, gate_hbm, up_hbm, down_hbm,
    out_ref,
    zbuf, xs, xr, gate_w, up_w, down_w, part, tbuf, trecv, ybuf, yrecv, cbuf, crecv, acc, held, handed,
    wsem, zsend_sem, zrecv_sem, xsend_sem, xrecv_sem, fsend_sem, frecv_sem,
    tsend_sem, trecv_sem, ysend_sem, yrecv_sem, csend_sem, crecv_sem, hand_sem,
):
    outer, inner, cap, picks, width, wide = sizes
    tok_count = tok_ref.shape[0]
    group = inner * cap
    e, c = lax.axis_index("expert"), lax.axis_index("tp")
    z, p = e // inner, e % inner
    other = 1 - c

    loads = [
        pltpu.make_async_copy(gate_hbm.at[0], gate_w, wsem.at[0]),
        pltpu.make_async_copy(up_hbm.at[0], up_w, wsem.at[1]),
        pltpu.make_async_copy(down_hbm.at[0], down_w, wsem.at[2]),
    ]
    for load in loads:
        load.start()

    barrier = pltpu.get_barrier_semaphore()
    for d in range(1, outer):
        pl.semaphore_signal(barrier, inc=1, device_id=((z + d) % outer * inner + p, c), device_id_type=MESH)
    for d in range(1, inner):
        pl.semaphore_signal(barrier, inc=1, device_id=(z * inner + flip(p, d, inner), c), device_id_type=MESH)
    pl.semaphore_signal(barrier, inc=1, device_id=(e, other), device_id_type=MESH)

    experts = outer * inner
    expert_lane = lax.broadcasted_iota(jnp.int32, (tok_count, experts), 1)
    square = (tok_count, tok_count)
    row_at, lane_at = lax.broadcasted_iota(jnp.int32, square, 0), lax.broadcasted_iota(jnp.int32, square, 1)

    def upright(line):
        return jnp.sum(jnp.where(row_at == lane_at, line, jnp.zeros_like(line)), axis=1, keepdims=True)

    chosen = [upright(ids_ref[k : k + 1, :]) for k in range(picks)]
    named = [(column == expert_lane).astype(F32) for column in chosen]
    lower = (lane_at < row_at).astype(F32)
    earlier = jnp.dot(lower, sum(named), preferred_element_type=F32)
    scores = jnp.exp(logit_ref[...])
    weights = scores / jnp.sum(scores, axis=0, keepdims=True)
    zbuf[z, :, wide - 128 :] = jnp.zeros((tok_count, 128), BF16)
    zbuf[z, :, :width] = tok_ref[...]
    tail = zbuf[z, :, wide - 128 :].astype(F32)
    lane = lax.broadcasted_iota(jnp.int32, (tok_count, 128), 1)
    first = 128 - 4 * picks
    for k in range(picks):
        slot = jnp.sum(earlier * named[k], axis=1, keepdims=True)
        weight = upright(weights[k : k + 1, :])
        high = weight.astype(BF16).astype(F32)
        for j, value in enumerate((chosen[k].astype(F32), slot, high, weight - high)):
            tail = jnp.where(lane == first + 4 * k + j, value, tail)
    zbuf[z, :, wide - 128 :] = tail.astype(BF16)

    pl.semaphore_wait(barrier, outer + inner - 1)

    def origin(s):
        near = jnp.minimum(z, outer - 1 - z)
        toward = jnp.where(2 * z < outer, -1, 1)
        j = (s + 1) // 2
        paired = jnp.where(s % 2 == 1, toward * j, -toward * j)
        return z + jnp.where(s <= 2 * near, paired, -toward * (s - near))

    def z_copy(block, way):
        return pltpu.make_async_remote_copy(
            src_ref=zbuf.at[block], dst_ref=zbuf.at[block],
            send_sem=zsend_sem.at[way, block], recv_sem=zrecv_sem.at[block],
            device_id=((z + 2 * way - 1) * inner + p, c), device_id_type=MESH,
        )

    def pass_on(d):
        @pl.when(z >= d)
        def _():
            z_copy(z - d, 1).wait_recv()

            @pl.when(z + 1 < outer)
            def _():
                z_copy(z - d, 1).start()

        @pl.when(z + d < outer)
        def _():
            z_copy(z + d, 0).wait_recv()

            @pl.when(z > 0)
            def _():
                z_copy(z + d, 0).start()

    def x_copy(s, d, receive=False):
        peer = flip(p, d, inner)
        return pltpu.make_async_remote_copy(
            src_ref=xs.at[s, peer], dst_ref=xr.at[s, c, peer if receive else p],
            send_sem=xsend_sem.at[s, d], recv_sem=xrecv_sem.at[s, d],
            device_id=(z * inner + peer, c), device_id_type=MESH,
        )

    def f_copy(s, d, receive=False):
        peer = flip(p, d, inner)
        return pltpu.make_async_remote_copy(
            src_ref=xr.at[s, c, peer], dst_ref=xr.at[s, other if receive else c, peer],
            send_sem=fsend_sem.at[s, d], recv_sem=frecv_sem.at[s, d],
            device_id=(e, other), device_id_type=MESH,
        )

    def t_copy(s):
        return pltpu.make_async_remote_copy(
            src_ref=tbuf.at[s], dst_ref=trecv.at[s], send_sem=tsend_sem.at[s], recv_sem=trecv_sem.at[s],
            device_id=(e, other), device_id_type=MESH,
        )

    def y_copy(s, d, receive=False):
        peer = flip(p, d, inner)
        return pltpu.make_async_remote_copy(
            src_ref=ybuf.at[s, peer], dst_ref=yrecv.at[s, peer if receive else p],
            send_sem=ysend_sem.at[s, d], recv_sem=yrecv_sem.at[s, d],
            device_id=(z * inner + peer, c), device_id_type=MESH,
        )

    def c_copy(s, peer, receive=False):
        return pltpu.make_async_remote_copy(
            src_ref=cbuf.at[s], dst_ref=crecv.at[peer if receive else z],
            send_sem=csend_sem.at[s], recv_sem=crecv_sem.at[peer if receive else z],
            device_id=(peer * inner + p, c), device_id_type=MESH,
        )

    mate = z + 1 - 2 * (z % 2)

    def hand_copy(s, block):
        return pltpu.make_async_remote_copy(
            src_ref=cbuf.at[s], dst_ref=handed.at[block],
            send_sem=csend_sem.at[s], recv_sem=hand_sem.at[block],
            device_id=(mate * inner + p, c), device_id_type=MESH,
        )

    def role(s):
        block = origin(s)
        within = block // 2 == z // 2
        nearer = jnp.where(block > z, z % 2 == 1, z % 2 == 0)
        return block, within, nearer

    def notes(s):
        told = zbuf[origin(s), :, wide - 128 :].astype(F32)
        found = []
        for k in range(picks):
            at = first + 4 * k
            row = told[:, at : at + 1] * cap + told[:, at + 1 : at + 2] - (z * group).astype(F32)
            found.append((row, told[:, at + 2 : at + 3], told[:, at + 3 : at + 4]))
        return found

    def slots():
        return lax.broadcasted_iota(jnp.int32, (tok_count, group), 1).astype(F32)

    def dispatch(s):
        rows = slots()
        placing = sum((row == rows).astype(F32) for row, _, _ in notes(s)).astype(BF16)
        packed = lax.dot_general(placing, zbuf[origin(s)], (((0,), (0,)), ((), ())), preferred_element_type=F32)
        xs[s] = packed.astype(BF16).reshape(inner, cap, wide)
        for d in range(1, inner):
            x_copy(s, d).start()
        xr[s, c, p] = xs[s, p]
        f_copy(s, 0).start()

    def compute(s):
        rows = xr[s, :, :, :, :width].reshape(2 * group, width)
        across = (((1,), (1,)), ((), ()))
        gate_act = lax.dot_general(rows, gate_w[...], across, preferred_element_type=F32)
        up_act = lax.dot_general(rows, up_w[...], across, preferred_element_type=F32)
        hidden = (gate_act * jax.nn.sigmoid(1.702 * gate_act) * (up_act + 1.0)).astype(BF16)
        part[s % 2] = jnp.dot(hidden, down_w[...], preferred_element_type=F32).reshape(2, group, width)
        tbuf[s] = part[s % 2, other].astype(BF16)
        t_copy(s).start()

    def give_back(s):
        t_copy(s).wait_recv()
        whole = part[s % 2, c] + trecv[s].astype(F32)
        ybuf[s] = whole.astype(BF16).reshape(inner, cap, width)
        for d in range(1, inner):
            y_copy(s, d).start()
        yrecv[s, p] = ybuf[s, p]

    def combine(s):
        for d in range(1, inner):
            y_copy(s, d, True).wait_recv()
        rows = slots()
        high = jnp.zeros((tok_count, group), F32)
        low = jnp.zeros((tok_count, group), F32)
        for row, weight_high, weight_low in notes(s):
            high = high + jnp.where(row == rows, weight_high, 0.0)
            low = low + jnp.where(row == rows, weight_low, 0.0)
        mixing = jnp.concatenate([high, low], axis=0).astype(BF16)
        both = jnp.dot(mixing, yrecv[s].reshape(group, width), preferred_element_type=F32)
        return both[:tok_count] + both[tok_count:]

    @pl.when(z + 1 < outer)
    def _():
        z_copy(z, 1).start()

    @pl.when(z > 0)
    def _():
        z_copy(z, 0).start()

    dispatch(0)

    def step(i, carry):
        @pl.when(i + 1 < outer)
        def _():
            pass_on(i + 1)
            dispatch(i + 1)

        @pl.when((i >= 1) & (i <= outer))
        def _():
            give_back(i - 1)

        @pl.when(i == 2)
        def _():
            acc[...] = combine(0)

        @pl.when(i > 2)
        def _():
            s = i - 2
            block, within, nearer = role(s)
            held[s] = combine(s)

            @pl.when(within)
            def _():
                cbuf[s] = held[s].astype(BF16)
                c_copy(s, block).start()

            @pl.when(jnp.logical_not(within) & jnp.logical_not(nearer))
            def _():
                cbuf[s] = held[s].astype(BF16)
                hand_copy(s, block).start()

        @pl.when(i < outer)
        def _():
            for d in range(1, inner):
                x_copy(i, d, True).wait_recv()
                f_copy(i, d).start()
            for d in range(inner):
                f_copy(i, d, True).wait_recv()

        @pl.when(i == 0)
        def _():
            for load in loads:
                load.wait()

        @pl.when(i < outer)
        def _():
            compute(i)

        return carry

    lax.fori_loop(0, outer + 2, step, 0)

    for s in range(1, outer):
        block, within, nearer = role(s)

        @pl.when(jnp.logical_not(within) & nearer)
        def _():
            hand_copy(s, block).wait_recv()
            cbuf[s] = (held[s] + handed[block].astype(F32)).astype(BF16)
            c_copy(s, block).start()

    total = acc[...]
    pairs = outer // 2
    for r in range(pairs):
        pair = (z // 2 + r) % pairs
        peer = mate if r == 0 else jnp.where(2 * pair > z, 2 * pair, 2 * pair + 1)
        c_copy(1, peer, True).wait_recv()
        total = total + crecv[peer].astype(F32)
    out_ref[...] = total.astype(BF16)

    for s in range(outer):
        for d in range(1, inner):
            x_copy(s, d).wait_send()
            y_copy(s, d).wait_send()
        for d in range(inner):
            f_copy(s, d).wait_send()
        t_copy(s).wait_send()
        if s > 0:
            c_copy(s, origin(s)).wait_send()

        @pl.when((s <= z) & (z + 1 < outer))
        def _():
            z_copy(s, 1).wait_send()

        @pl.when((s >= z) & (z > 0))
        def _():
            z_copy(s, 0).wait_send()


def split_of(experts):
    inner = 1
    while 4 * inner * inner <= experts:
        inner *= 2
    return experts // inner, inner


def fused_plan(mesh, tokens, expert_ids, gate_weight):
    experts, cores = mesh.shape["expert"], mesh.shape["tp"]
    tok_dev, width = tokens.shape
    picks, half = expert_ids.shape[1], gate_weight.shape[2]
    cap = 2 * tok_dev * picks // experts
    outer, inner = split_of(experts)
    wide = -(-(width + 4 * picks) // 128) * 128
    if cores != 2 or outer * inner != experts or experts & (experts - 1) or experts > 256:
        return None
    if cap % 16 or tok_dev % 16 or tok_dev > 256 or width % 16 or half % 16:
        return None
    rows = outer * inner * cap
    held = 2 * wide * (3 * half + 7 * rows + 6 * outer * tok_dev) + 16 * wide * inner * cap
    if held > 44 * 2**20:
        return None
    return outer, inner, cap, picks, width, wide


def fused(sizes, tokens, expert_ids, route_logits, gate_weight, up_weight, down_weight):
    outer, inner, cap, picks, width, wide = sizes
    tok_dev = tokens.shape[0]
    half = gate_weight.shape[2]
    group = inner * cap
    gate, up = gate_weight.swapaxes(1, 2), up_weight.swapaxes(1, 2)
    vmem, hbm = pl.BlockSpec(memory_space=pltpu.VMEM), pl.BlockSpec(memory_space=pl.ANY)
    dma = pltpu.SemaphoreType.DMA
    rows = 2 * outer * group
    return pl.pallas_call(
        functools.partial(moe_kernel, sizes),
        out_shape=jax.ShapeDtypeStruct((tok_dev, width), BF16),
        in_specs=[vmem, vmem, vmem, hbm, hbm, hbm],
        out_specs=vmem,
        scratch_shapes=[
            pltpu.VMEM((outer, tok_dev, wide), BF16),
            pltpu.VMEM((outer, inner, cap, wide), BF16),
            pltpu.VMEM((outer, 2, inner, cap, wide), BF16),
            pltpu.VMEM((half, width), BF16),
            pltpu.VMEM((half, width), BF16),
            pltpu.VMEM((half, width), BF16),
            pltpu.VMEM((2, 2, group, width), F32),
            pltpu.VMEM((outer, group, width), BF16),
            pltpu.VMEM((outer, group, width), BF16),
            pltpu.VMEM((outer, inner, cap, width), BF16),
            pltpu.VMEM((outer, inner, cap, width), BF16),
            pltpu.VMEM((outer, tok_dev, width), BF16),
            pltpu.VMEM((outer, tok_dev, width), BF16),
            pltpu.VMEM((tok_dev, width), F32),
            pltpu.VMEM((outer, tok_dev, width), F32),
            pltpu.VMEM((outer, tok_dev, width), BF16),
            dma((3,)),
            dma((2, outer)), dma((outer,)),
            dma((outer, inner)), dma((outer, inner)),
            dma((outer, inner)), dma((outer, inner)),
            dma((outer,)), dma((outer,)),
            dma((outer, inner)), dma((outer, inner)),
            dma((outer,)), dma((outer,)), dma((outer,)),
        ],
        compiler_params=pltpu.CompilerParams(
            collective_id=0, has_side_effects=True, vmem_limit_bytes=56 * 2**20
        ),
        cost_estimate=pl.CostEstimate(
            flops=6 * rows * width * half, bytes_accessed=6 * width * half, transcendentals=rows * half
        ),
    )(tokens, expert_ids.T, route_logits.T, gate, up, down_weight)


def plain(tokens, expert_ids, route_logits, gate_weight, up_weight, down_weight):
    experts = lax.axis_size("expert")
    tok_dev, model_width = tokens.shape
    pick_count = expert_ids.shape[1]
    capacity = 2 * tok_dev * pick_count // experts
    flat_ids = expert_ids.reshape(-1)
    pick_range = jnp.arange(flat_ids.shape[0], dtype=jnp.int32)
    same = (flat_ids[:, None] == flat_ids[None, :]) & (pick_range[None, :] < pick_range[:, None])
    slot_index = jnp.sum(same.astype(jnp.int32), axis=1)
    position = flat_ids * capacity + slot_index
    slot_range = jnp.arange(experts * capacity, dtype=jnp.int32)
    matches = (position[:, None] == slot_range[None, :]).astype(jnp.int32)
    placing = jnp.sum(matches.reshape(tok_dev, pick_count, -1), axis=1).astype(jnp.bfloat16)
    outgoing = lax.dot_general(
        placing, tokens, (((0,), (0,)), ((), ())), preferred_element_type=jnp.float32
    )
    outgoing = outgoing.astype(jnp.bfloat16).reshape(experts, capacity, model_width)
    gate_local = gate_weight[0]
    up_local = up_weight[0]
    down_local = down_weight[0]
    received = lax.all_to_all(outgoing, "expert", split_axis=0, concat_axis=0, tiled=True)
    items = received.shape[1]
    row_total = experts * items
    row_block = received.reshape(row_total, model_width)
    paired = lax.all_gather(row_block, "tp", axis=0, tiled=True)
    gate_act = jnp.dot(paired, gate_local, preferred_element_type=jnp.float32)
    up_act = jnp.dot(paired, up_local, preferred_element_type=jnp.float32)
    hidden = (gate_act * jax.nn.sigmoid(1.702 * gate_act) * (up_act + 1.0)).astype(jnp.bfloat16)
    summed = lax.psum_scatter(
        jnp.dot(hidden, down_local, preferred_element_type=jnp.float32),
        "tp",
        scatter_dimension=0,
        tiled=True,
    )
    results = summed.astype(jnp.bfloat16).reshape(experts, items, model_width)
    returned = lax.all_to_all(results, "expert", split_axis=0, concat_axis=0, tiled=True).reshape(
        experts * capacity, model_width
    )
    picked = returned[position.reshape(tok_dev, pick_count)]
    scores = jnp.exp(route_logits)
    weights = scores / jnp.sum(scores, axis=1, keepdims=True)
    mixed_out = jnp.sum(weights[:, :, None] * picked.astype(jnp.float32), axis=1)
    return mixed_out.astype(jnp.bfloat16)


def solution(mesh):
    def body(tokens, expert_ids, route_logits, gate_weight, up_weight, down_weight):
        sizes = fused_plan(mesh, tokens, expert_ids, gate_weight)
        run = plain if sizes is None else functools.partial(fused, sizes)
        return run(tokens, expert_ids, route_logits, gate_weight, up_weight, down_weight)

    placed = (
        P(("expert", "tp"), None),
        P(("expert", "tp"), None),
        P(("expert", "tp"), None),
        P("expert", None, "tp"),
        P("expert", None, "tp"),
        P("expert", "tp", None),
    )
    return jax.shard_map(
        body, mesh=mesh, in_specs=placed, out_specs=P(("expert", "tp"), None), check_vma=False
    )
```

```python
import functools

import jax
import jax.numpy as jnp
from jax import lax
from jax.experimental import pallas as pl
from jax.experimental.pallas import tpu as pltpu
from jax.sharding import PartitionSpec as P

MESH = pl.DeviceIdType.MESH
F32 = jnp.float32
BF16 = jnp.bfloat16


def flip(a, b, extent):
    total, bit = 0, 1
    while bit < extent:
        total = total + ((a // bit + b // bit) % 2) * bit
        bit *= 2
    return total


def moe_kernel(
    sizes,
    tok_ref, ids_ref, logit_ref, gate_hbm, up_hbm, down_hbm,
    out_ref,
    zbuf, xs, xr, gate_w, up_w, down_w, part, tbuf, trecv, ybuf, yrecv, cbuf, crecv, held, handed,
    wsem, zsend_sem, zrecv_sem, xsend_sem, xrecv_sem, fsend_sem, frecv_sem,
    tsend_sem, trecv_sem, ysend_sem, yrecv_sem, csend_sem, crecv_sem, hand_sem,
):
    outer, inner, cap, picks, width, wide = sizes
    tok_count = tok_ref.shape[0]
    group = inner * cap
    e, c = lax.axis_index("expert"), lax.axis_index("tp")
    z, p = e // inner, e % inner
    other = 1 - c

    loads = [
        pltpu.make_async_copy(gate_hbm.at[0], gate_w, wsem.at[0]),
        pltpu.make_async_copy(up_hbm.at[0], up_w, wsem.at[1]),
        pltpu.make_async_copy(down_hbm.at[0], down_w, wsem.at[2]),
    ]
    for load in loads:
        load.start()

    barrier = pltpu.get_barrier_semaphore()
    for d in range(1, outer):
        pl.semaphore_signal(barrier, inc=1, device_id=((z + d) % outer * inner + p, c), device_id_type=MESH)
    for d in range(1, inner):
        pl.semaphore_signal(barrier, inc=1, device_id=(z * inner + flip(p, d, inner), c), device_id_type=MESH)
    pl.semaphore_signal(barrier, inc=1, device_id=(e, other), device_id_type=MESH)

    experts = outer * inner
    expert_lane = lax.broadcasted_iota(jnp.int32, (tok_count, experts), 1)
    square = (tok_count, tok_count)
    row_at, lane_at = lax.broadcasted_iota(jnp.int32, square, 0), lax.broadcasted_iota(jnp.int32, square, 1)

    def upright(line):
        return jnp.sum(jnp.where(row_at == lane_at, line, jnp.zeros_like(line)), axis=1, keepdims=True)

    chosen = [upright(ids_ref[k : k + 1, :]) for k in range(picks)]
    named = [(column == expert_lane).astype(F32) for column in chosen]
    lower = (lane_at < row_at).astype(F32)
    earlier = jnp.dot(lower, sum(named), preferred_element_type=F32)
    scores = jnp.exp(logit_ref[...])
    weights = scores / jnp.sum(scores, axis=0, keepdims=True)
    zbuf[z, :, wide - 128 :] = jnp.zeros((tok_count, 128), BF16)
    zbuf[z, :, :width] = tok_ref[...]
    tail = zbuf[z, :, wide - 128 :].astype(F32)
    lane = lax.broadcasted_iota(jnp.int32, (tok_count, 128), 1)
    first = 128 - 4 * picks
    for k in range(picks):
        slot = jnp.sum(earlier * named[k], axis=1, keepdims=True)
        weight = upright(weights[k : k + 1, :])
        high = weight.astype(BF16).astype(F32)
        for j, value in enumerate((chosen[k].astype(F32), slot, high, weight - high)):
            tail = jnp.where(lane == first + 4 * k + j, value, tail)
    zbuf[z, :, wide - 128 :] = tail.astype(BF16)

    pl.semaphore_wait(barrier, outer + inner - 1)

    def origin(s):
        near = jnp.minimum(z, outer - 1 - z)
        toward = jnp.where(2 * z < outer, -1, 1)
        turn = (s + 1) % outer
        j = (turn + 1) // 2
        paired = jnp.where(turn % 2 == 1, toward * j, -toward * j)
        return z + jnp.where(turn <= 2 * near, paired, -toward * (turn - near))

    def z_copy(block, way):
        return pltpu.make_async_remote_copy(
            src_ref=zbuf.at[block], dst_ref=zbuf.at[block],
            send_sem=zsend_sem.at[way, block], recv_sem=zrecv_sem.at[block],
            device_id=((z + 2 * way - 1) * inner + p, c), device_id_type=MESH,
        )

    def pass_on(d):
        @pl.when(z >= d)
        def _():
            z_copy(z - d, 1).wait_recv()

            @pl.when(z + 1 < outer)
            def _():
                z_copy(z - d, 1).start()

        @pl.when(z + d < outer)
        def _():
            z_copy(z + d, 0).wait_recv()

            @pl.when(z > 0)
            def _():
                z_copy(z + d, 0).start()

    def x_copy(s, d, receive=False):
        peer = flip(p, d, inner)
        return pltpu.make_async_remote_copy(
            src_ref=xs.at[s, peer], dst_ref=xr.at[s, c, peer if receive else p],
            send_sem=xsend_sem.at[s, d], recv_sem=xrecv_sem.at[s, d],
            device_id=(z * inner + peer, c), device_id_type=MESH,
        )

    def f_copy(s, d, receive=False):
        peer = flip(p, d, inner)
        return pltpu.make_async_remote_copy(
            src_ref=xr.at[s, c, peer], dst_ref=xr.at[s, other if receive else c, peer],
            send_sem=fsend_sem.at[s, d], recv_sem=frecv_sem.at[s, d],
            device_id=(e, other), device_id_type=MESH,
        )

    def t_copy(s):
        return pltpu.make_async_remote_copy(
            src_ref=tbuf.at[s], dst_ref=trecv.at[s], send_sem=tsend_sem.at[s], recv_sem=trecv_sem.at[s],
            device_id=(e, other), device_id_type=MESH,
        )

    def y_copy(s, d, receive=False):
        peer = flip(p, d, inner)
        return pltpu.make_async_remote_copy(
            src_ref=ybuf.at[s, peer], dst_ref=yrecv.at[s, peer if receive else p],
            send_sem=ysend_sem.at[s, d], recv_sem=yrecv_sem.at[s, d],
            device_id=(z * inner + peer, c), device_id_type=MESH,
        )

    def c_copy(s, peer, receive=False):
        return pltpu.make_async_remote_copy(
            src_ref=cbuf.at[s], dst_ref=crecv.at[peer if receive else z],
            send_sem=csend_sem.at[s], recv_sem=crecv_sem.at[peer if receive else z],
            device_id=(peer * inner + p, c), device_id_type=MESH,
        )

    mate = z + 1 - 2 * (z % 2)

    def hand_copy(s, block):
        return pltpu.make_async_remote_copy(
            src_ref=cbuf.at[s], dst_ref=handed.at[block],
            send_sem=csend_sem.at[s], recv_sem=hand_sem.at[block],
            device_id=(mate * inner + p, c), device_id_type=MESH,
        )

    def role(s):
        block = origin(s)
        within = block // 2 == z // 2
        nearer = jnp.where(block > z, z % 2 == 1, z % 2 == 0)
        return block, within, nearer

    def notes(s):
        told = zbuf[origin(s), :, wide - 128 :].astype(F32)
        found = []
        for k in range(picks):
            at = first + 4 * k
            row = told[:, at : at + 1] * cap + told[:, at + 1 : at + 2] - (z * group).astype(F32)
            found.append((row, told[:, at + 2 : at + 3], told[:, at + 3 : at + 4]))
        return found

    def slots():
        return lax.broadcasted_iota(jnp.int32, (tok_count, group), 1).astype(F32)

    def dispatch(s):
        rows = slots()
        placing = sum((row == rows).astype(F32) for row, _, _ in notes(s)).astype(BF16)
        packed = lax.dot_general(placing, zbuf[origin(s)], (((0,), (0,)), ((), ())), preferred_element_type=F32)
        xs[s] = packed.astype(BF16).reshape(inner, cap, wide)
        for d in range(1, inner):
            x_copy(s, d).start()
        xr[s, c, p] = xs[s, p]
        f_copy(s, 0).start()

    def compute(s):
        rows = xr[s, :, :, :, :width].reshape(2 * group, width)
        across = (((1,), (1,)), ((), ()))
        gate_act = lax.dot_general(rows, gate_w[...], across, preferred_element_type=F32)
        up_act = lax.dot_general(rows, up_w[...], across, preferred_element_type=F32)
        hidden = (gate_act * jax.nn.sigmoid(1.702 * gate_act) * (up_act + 1.0)).astype(BF16)
        part[s % 2] = jnp.dot(hidden, down_w[...], preferred_element_type=F32).reshape(2, group, width)
        tbuf[s] = part[s % 2, other].astype(BF16)
        t_copy(s).start()

    def give_back(s):
        t_copy(s).wait_recv()
        whole = part[s % 2, c] + trecv[s].astype(F32)
        ybuf[s] = whole.astype(BF16).reshape(inner, cap, width)
        for d in range(1, inner):
            y_copy(s, d).start()
        yrecv[s, p] = ybuf[s, p]

    def combine(s):
        for d in range(1, inner):
            y_copy(s, d, True).wait_recv()
        rows = slots()
        high = jnp.zeros((tok_count, group), F32)
        low = jnp.zeros((tok_count, group), F32)
        for row, weight_high, weight_low in notes(s):
            high = high + jnp.where(row == rows, weight_high, 0.0)
            low = low + jnp.where(row == rows, weight_low, 0.0)
        mixing = jnp.concatenate([high, low], axis=0).astype(BF16)
        both = jnp.dot(mixing, yrecv[s].reshape(group, width), preferred_element_type=F32)
        return both[:tok_count] + both[tok_count:]

    @pl.when(z + 1 < outer)
    def _():
        z_copy(z, 1).start()

    @pl.when(z > 0)
    def _():
        z_copy(z, 0).start()

    dispatch(outer - 1)
    if outer > 1:
        pass_on(1)
        dispatch(0)

    def step(i, carry):
        @pl.when(i + 2 < outer)
        def _():
            pass_on(i + 2)
            dispatch(i + 1)

        @pl.when((i >= 1) & (i <= outer))
        def _():
            give_back(i - 1)

        @pl.when((i >= 2) & (i <= outer))
        def _():
            s = i - 2
            block, within, nearer = role(s)
            held[s] = combine(s)

            @pl.when(within)
            def _():
                cbuf[s] = held[s].astype(BF16)
                c_copy(s, block).start()

            @pl.when(jnp.logical_not(within) & jnp.logical_not(nearer))
            def _():
                cbuf[s] = held[s].astype(BF16)
                hand_copy(s, block).start()

        @pl.when(i < outer)
        def _():
            for d in range(1, inner):
                x_copy(i, d, True).wait_recv()
                f_copy(i, d).start()
            for d in range(inner):
                f_copy(i, d, True).wait_recv()

        @pl.when(i == 0)
        def _():
            for load in loads:
                load.wait()

        @pl.when(i < outer)
        def _():
            compute(i)

        return carry

    lax.fori_loop(0, outer + 1, step, 0)

    for s in range(outer - 1):
        block, within, nearer = role(s)

        @pl.when(jnp.logical_not(within) & nearer)
        def _():
            hand_copy(s, block).wait_recv()
            cbuf[s] = (held[s] + handed[block].astype(F32)).astype(BF16)
            c_copy(s, block).start()

    total = combine(outer - 1)
    pairs = outer // 2
    for r in range(pairs):
        pair = (z // 2 + r) % pairs
        peer = mate if r == 0 else jnp.where(2 * pair > z, 2 * pair, 2 * pair + 1)
        c_copy(0, peer, True).wait_recv()
        total = total + crecv[peer].astype(F32)
    out_ref[...] = total.astype(BF16)

    for s in range(outer):
        for d in range(1, inner):
            x_copy(s, d).wait_send()
            y_copy(s, d).wait_send()
        for d in range(inner):
            f_copy(s, d).wait_send()
        t_copy(s).wait_send()
        if s < outer - 1:
            c_copy(s, origin(s)).wait_send()

        @pl.when((s <= z) & (z + 1 < outer))
        def _():
            z_copy(s, 1).wait_send()

        @pl.when((s >= z) & (z > 0))
        def _():
            z_copy(s, 0).wait_send()


def split_of(experts):
    inner = 1
    while 4 * inner * inner <= experts:
        inner *= 2
    return experts // inner, inner


def fused_plan(mesh, tokens, expert_ids, gate_weight):
    experts, cores = mesh.shape["expert"], mesh.shape["tp"]
    tok_dev, width = tokens.shape
    picks, half = expert_ids.shape[1], gate_weight.shape[2]
    cap = 2 * tok_dev * picks // experts
    outer, inner = split_of(experts)
    wide = -(-(width + 4 * picks) // 128) * 128
    if cores != 2 or outer * inner != experts or experts & (experts - 1) or experts > 256:
        return None
    if cap % 16 or tok_dev % 16 or tok_dev > 256 or width % 16 or half % 16:
        return None
    rows = outer * inner * cap
    held = 2 * wide * (3 * half + 7 * rows + 6 * outer * tok_dev) + 16 * wide * inner * cap
    if held > 44 * 2**20:
        return None
    return outer, inner, cap, picks, width, wide


def fused(sizes, tokens, expert_ids, route_logits, gate_weight, up_weight, down_weight):
    outer, inner, cap, picks, width, wide = sizes
    tok_dev = tokens.shape[0]
    half = gate_weight.shape[2]
    group = inner * cap
    gate, up = gate_weight.swapaxes(1, 2), up_weight.swapaxes(1, 2)
    vmem, hbm = pl.BlockSpec(memory_space=pltpu.VMEM), pl.BlockSpec(memory_space=pl.ANY)
    dma = pltpu.SemaphoreType.DMA
    rows = 2 * outer * group
    return pl.pallas_call(
        functools.partial(moe_kernel, sizes),
        out_shape=jax.ShapeDtypeStruct((tok_dev, width), BF16),
        in_specs=[vmem, vmem, vmem, hbm, hbm, hbm],
        out_specs=vmem,
        scratch_shapes=[
            pltpu.VMEM((outer, tok_dev, wide), BF16),
            pltpu.VMEM((outer, inner, cap, wide), BF16),
            pltpu.VMEM((outer, 2, inner, cap, wide), BF16),
            pltpu.VMEM((half, width), BF16),
            pltpu.VMEM((half, width), BF16),
            pltpu.VMEM((half, width), BF16),
            pltpu.VMEM((2, 2, group, width), F32),
            pltpu.VMEM((outer, group, width), BF16),
            pltpu.VMEM((outer, group, width), BF16),
            pltpu.VMEM((outer, inner, cap, width), BF16),
            pltpu.VMEM((outer, inner, cap, width), BF16),
            pltpu.VMEM((outer, tok_dev, width), BF16),
            pltpu.VMEM((outer, tok_dev, width), BF16),
            pltpu.VMEM((outer, tok_dev, width), F32),
            pltpu.VMEM((outer, tok_dev, width), BF16),
            dma((3,)),
            dma((2, outer)), dma((outer,)),
            dma((outer, inner)), dma((outer, inner)),
            dma((outer, inner)), dma((outer, inner)),
            dma((outer,)), dma((outer,)),
            dma((outer, inner)), dma((outer, inner)),
            dma((outer,)), dma((outer,)), dma((outer,)),
        ],
        compiler_params=pltpu.CompilerParams(
            collective_id=0, has_side_effects=True, vmem_limit_bytes=56 * 2**20
        ),
        cost_estimate=pl.CostEstimate(
            flops=6 * rows * width * half, bytes_accessed=6 * width * half, transcendentals=rows * half
        ),
    )(tokens, expert_ids.T, route_logits.T, gate, up, down_weight)


def plain(tokens, expert_ids, route_logits, gate_weight, up_weight, down_weight):
    experts = lax.axis_size("expert")
    tok_dev, model_width = tokens.shape
    pick_count = expert_ids.shape[1]
    capacity = 2 * tok_dev * pick_count // experts
    flat_ids = expert_ids.reshape(-1)
    pick_range = jnp.arange(flat_ids.shape[0], dtype=jnp.int32)
    same = (flat_ids[:, None] == flat_ids[None, :]) & (pick_range[None, :] < pick_range[:, None])
    slot_index = jnp.sum(same.astype(jnp.int32), axis=1)
    position = flat_ids * capacity + slot_index
    slot_range = jnp.arange(experts * capacity, dtype=jnp.int32)
    matches = (position[:, None] == slot_range[None, :]).astype(jnp.int32)
    placing = jnp.sum(matches.reshape(tok_dev, pick_count, -1), axis=1).astype(jnp.bfloat16)
    outgoing = lax.dot_general(
        placing, tokens, (((0,), (0,)), ((), ())), preferred_element_type=jnp.float32
    )
    outgoing = outgoing.astype(jnp.bfloat16).reshape(experts, capacity, model_width)
    gate_local = gate_weight[0]
    up_local = up_weight[0]
    down_local = down_weight[0]
    received = lax.all_to_all(outgoing, "expert", split_axis=0, concat_axis=0, tiled=True)
    items = received.shape[1]
    row_total = experts * items
    row_block = received.reshape(row_total, model_width)
    paired = lax.all_gather(row_block, "tp", axis=0, tiled=True)
    gate_act = jnp.dot(paired, gate_local, preferred_element_type=jnp.float32)
    up_act = jnp.dot(paired, up_local, preferred_element_type=jnp.float32)
    hidden = (gate_act * jax.nn.sigmoid(1.702 * gate_act) * (up_act + 1.0)).astype(jnp.bfloat16)
    summed = lax.psum_scatter(
        jnp.dot(hidden, down_local, preferred_element_type=jnp.float32),
        "tp",
        scatter_dimension=0,
        tiled=True,
    )
    results = summed.astype(jnp.bfloat16).reshape(experts, items, model_width)
    returned = lax.all_to_all(results, "expert", split_axis=0, concat_axis=0, tiled=True).reshape(
        experts * capacity, model_width
    )
    picked = returned[position.reshape(tok_dev, pick_count)]
    scores = jnp.exp(route_logits)
    weights = scores / jnp.sum(scores, axis=1, keepdims=True)
    mixed_out = jnp.sum(weights[:, :, None] * picked.astype(jnp.float32), axis=1)
    return mixed_out.astype(jnp.bfloat16)


def solution(mesh):
    def body(tokens, expert_ids, route_logits, gate_weight, up_weight, down_weight):
        sizes = fused_plan(mesh, tokens, expert_ids, gate_weight)
        run = plain if sizes is None else functools.partial(fused, sizes)
        return run(tokens, expert_ids, route_logits, gate_weight, up_weight, down_weight)

    placed = (
        P(("expert", "tp"), None),
        P(("expert", "tp"), None),
        P(("expert", "tp"), None),
        P("expert", None, "tp"),
        P("expert", None, "tp"),
        P("expert", "tp", None),
    )
    return jax.shard_map(
        body, mesh=mesh, in_specs=placed, out_specs=P(("expert", "tp"), None), check_vma=False
    )
```
